32 devices in a mesh: img: 4 (over y, core), gz: 8 (over z, x).
Axes of the slice: x: 2, y: 2, z: 4, core: 2. Of those that a mesh axis runs over, the one named last changes fastest.
Arguments:
- images: float32 [16, 5, 16, 128, 128], P('img', None, 'gz'), may hold values from -12 to 12
- centre: int32 [16], P('img'), may hold values from 1 to 14, as said below
- positions: float32 [16], P('img'), may hold values from 0 to 1
Outputs:
- path: float32 [16, 5, 16, 128, 128], P('img', None, 'gz')
The draws below stay inside these ranges and needn't reach their ends.
Inputs may be any that keep to these rules, and one draw needn't show every extreme that they name: `centre`: centre_m lies within m - 1 to m + 1, clipped to 1 to 14; at the first target of each aligned block of 4 it is m - 1 and at the last m + 1, before clipping.
All inputs are finite; a program needn't handle non-finite values.
Results may differ from the reference program's by a relative error of at most 0.0003.
Values sent between devices are 32-bit elements; how exact they have to be, the bound alone decides.
A program may use at most 64 MiB of HBM per device.

```python
import math
import jax
import jax.numpy as jnp
from jax import lax

NX = 128
NY = 128
IMG_DEV = 4
IMAGES = 16
NZ = 16


def draw_images(key, part):
    shape = (IMAGES, 5, NZ, NX, NY)
    noise_key = jax.random.fold_in(key, 11)
    scale_key = jax.random.fold_in(key, 12)
    base = jnp.clip(jax.random.normal(noise_key, shape, jnp.float32), -5.0, 5.0)
    per_image = jax.random.uniform(scale_key, (IMAGES,), jnp.float32, 0.7, 1.3)
    planes = jnp.arange(NZ, dtype=jnp.int32).astype(jnp.float32)
    ramp = 1.0 + 0.75 * planes / (NZ - 1)
    field = base * per_image[:, None, None, None, None] * ramp[None, None, :, None, None]
    return field


def draw_centre(key, part):
    offsets = jax.random.randint(jax.random.fold_in(key, 21), (IMAGES,), -1, 2)
    index = jnp.arange(IMAGES, dtype=jnp.int32)
    local = index % IMG_DEV
    offsets = jnp.where(local == 0, -1, jnp.where(local == IMG_DEV - 1, 1, offsets))
    return jnp.clip(index + offsets, 1, IMAGES - 2).astype(jnp.int32)


def draw_positions(key, part):
    jitter = jax.random.uniform(jax.random.fold_in(key, 31), (IMAGES,), jnp.float32, -0.3, 0.3)
    index = jnp.arange(IMAGES, dtype=jnp.int32).astype(jnp.float32)
    return jnp.clip((index + jitter) / (IMAGES - 1), 0.0, 1.0)


def setup_inputs(seed: int = 0) -> dict:
    keys = jax.random.split(jax.random.key(seed), 4)
    images = draw_images(jax.random.fold_in(keys[3], 71), 0)
    centre = draw_centre(jax.random.fold_in(keys[3], 71), 0)
    positions = draw_positions(jax.random.fold_in(keys[3], 71), 0)
    return dict(images=images, centre=centre, positions=positions)


elastic = 1.0
chiral_weight = 0.5
bulk_linear = -0.2
bulk_cubic = 0.5
bulk_quartic = 0.1
step_size = 1.0
smoothing = 64.0
epsilon = 1e-06
slot_pairs = ((0, 0), (0, 1), (0, 2), (1, 1), (1, 2))
slot_index = {(0, 0): 0, (0, 1): 1, (0, 2): 2, (1, 1): 3, (1, 2): 4}

def levi(first, middle, last):
    return (first - middle) * (middle - last) * (last - first) // 2

def tensor_entry(fields, row, column):
    if row > column:
        row, column = (column, row)
    if row == 2:
        return -(fields[0] + fields[3])
    return fields[slot_index[row, column]]

def nonlinear_drive(padded):
    fields_pad = [padded[:, slot] for slot in range(5)]
    centre_fields = [field[:, 1:-1] for field in fields_pad]
    grad_x = [(jnp.roll(field, -1, 2) - jnp.roll(field, 1, 2)) * 0.5 for field in centre_fields]
    grad_y = [(jnp.roll(field, -1, 3) - jnp.roll(field, 1, 3)) * 0.5 for field in centre_fields]
    grad_z = [(field[:, 2:] - field[:, :-2]) * 0.5 for field in fields_pad]
    gradients = (grad_x, grad_y, grad_z)
    laplace = []
    for field, inner in zip(fields_pad, centre_fields):
        value = field[:, 2:] + field[:, :-2] + jnp.roll(inner, 1, 2) + jnp.roll(inner, -1, 2)
        value = value + jnp.roll(inner, 1, 3) + jnp.roll(inner, -1, 3) - 6.0 * inner
        laplace.append(value)

    def curl_entry(row, column):
        total = jnp.zeros_like(centre_fields[0])
        for middle in range(3):
            for last in range(3):
                sign = levi(row, middle, last)
                if sign != 0:
                    total = total + sign * tensor_entry(gradients[middle], last, column)
        return total

    def square_entry(row, column):
        total = jnp.zeros_like(centre_fields[0])
        for middle in range(3):
            total = total + tensor_entry(centre_fields, row, middle) * tensor_entry(centre_fields, middle, column)
        return total
    trace = square_entry(0, 0) + square_entry(1, 1) + square_entry(2, 2)
    results = []
    for slot, pair in enumerate(slot_pairs):
        row, column = pair
        value = centre_fields[slot]
        chiral = curl_entry(row, column) + curl_entry(column, row)
        square = square_entry(row, column)
        if row == column:
            square = square - trace / 3.0
        bulk = bulk_linear * value - bulk_cubic * square + bulk_quartic * trace * value
        results.append(elastic * laplace[slot] - chiral_weight * chiral - bulk)
    return jnp.stack(results, axis=1)

def symbol_line(wave, length):
    return 2.0 - 2.0 * jnp.cos(2.0 * math.pi / length * wave.astype(jnp.float32))

def interp_matrix(arc, centre, target, columns, offset):
    nodes_index = jnp.arange(arc.shape[0], dtype=jnp.int32)

    def pick(where_at):
        return lax.optimization_barrier(jnp.sum(arc[None, :] * (nodes_index[None, :] == where_at[:, None]).astype(jnp.float32), axis=1))
    before = pick(centre - 1)
    middle = pick(centre)
    after = pick(centre + 1)
    weight_before = (target - middle) * (target - after) / ((before - middle) * (before - after))
    weight_middle = (target - before) * (target - after) / ((middle - before) * (middle - after))
    weight_after = (target - before) * (target - middle) / ((after - before) * (after - middle))
    column_index = jnp.arange(columns, dtype=jnp.int32)
    matrix = jnp.zeros((centre.shape[0], columns), jnp.float32)
    for shift_by, weight in ((-1, weight_before), (0, weight_middle), (1, weight_after)):
        spot = centre + shift_by - offset
        matrix = matrix + weight[:, None] * (column_index[None, :] == spot[:, None]).astype(jnp.float32)
    return matrix

def reference(images, centre, positions):
    symbol = symbol_line(jnp.arange(NZ, dtype=jnp.int32), NZ)[:, None, None]
    symbol = symbol + symbol_line(jnp.arange(NX, dtype=jnp.int32), NX)[None, :, None]
    symbol = symbol + symbol_line(jnp.arange(NY, dtype=jnp.int32), NY)[None, None, :]
    multiplier = step_size / (1.0 + smoothing * symbol)

    def advance(image):
        padded = jnp.concatenate([image[:, -1:], image, image[:, :1]], axis=1)
        drive = nonlinear_drive(padded[None])[0]
        spectrum = jnp.fft.fftn(drive, axes=(1, 2, 3))
        return image + jnp.real(jnp.fft.ifftn(spectrum * multiplier, axes=(1, 2, 3)))
    stepped = lax.map(advance, images)

    def gap_sum(index):
        gap = stepped[index + 1] - stepped[index]
        return jnp.sum(gap * gap)
    squares = lax.map(gap_sum, jnp.arange(IMAGES - 1, dtype=jnp.int32))
    cells = 5.0 * NZ * NX * NY
    dist = jnp.concatenate([jnp.sqrt(squares / cells + epsilon), jnp.zeros((1,), jnp.float32)])
    arc = jnp.cumsum(dist) - dist
    target = positions * arc[-1]
    matrix = interp_matrix(arc, centre, target, IMAGES, jnp.zeros((), jnp.int32))
    return jnp.einsum('mr,rqzxy->mqzxy', matrix, stepped, precision=lax.Precision.HIGHEST)
```

```python
import math

import jax
import jax.numpy as jnp
from jax import lax
from jax.sharding import PartitionSpec as P

elastic = 1.0
chiral_weight = 0.5
bulk_linear = -0.2
bulk_cubic = 0.5
bulk_quartic = 0.1
step_size = 1.0
smoothing = 64.0
epsilon = 1e-06
chunks = 2


def shift_along(block, axis, step, periodic):
    count = lax.axis_size(axis)
    pairs = [(i, i + step) for i in range(count) if 0 <= i + step < count]
    if periodic:
        pairs = [(i, (i + step) % count) for i in range(count)]
    return lax.ppermute(block, axis, pairs)


def z_sources(images):
    return jnp.stack(
        [images[:, 1], images[:, 2], images[:, 4], images[:, 0] - images[:, 3]], axis=1
    )


def local_drive(images, low, high):
    q1, q2, q3, q4, q5 = (images[:, slot] for slot in range(5))
    q6 = -(q1 + q4)

    def grad_x(field):
        return (jnp.roll(field, -1, 2) - jnp.roll(field, 1, 2)) * 0.5

    def grad_y(field):
        return (jnp.roll(field, -1, 3) - jnp.roll(field, 1, 3)) * 0.5

    def grad_z(field, slot):
        padded = jnp.concatenate([low[:, slot], field, high[:, slot]], axis=1)
        return (padded[:, 2:] - padded[:, :-2]) * 0.5

    z2 = grad_z(q2, 0)
    z3 = grad_z(q3, 1)
    z5 = grad_z(q5, 2)
    z14 = grad_z(q1 - q4, 3)
    chiral = (
        2.0 * (grad_y(q3) - z2),
        grad_y(q5) - grad_x(q3) + z14,
        grad_y(q6 - q1) + grad_x(q2) - z5,
        2.0 * (z2 - grad_x(q5)),
        z3 + grad_x(q4 - q6) - grad_y(q2),
    )
    s1 = q1 * q1 + q2 * q2 + q3 * q3
    s4 = q2 * q2 + q4 * q4 + q5 * q5
    trace = s1 + s4 + q3 * q3 + q5 * q5 + q6 * q6
    square = (
        s1 - trace / 3.0,
        q1 * q2 + q2 * q4 + q3 * q5,
        q1 * q3 + q2 * q5 + q3 * q6,
        s4 - trace / 3.0,
        q2 * q3 + q4 * q5 + q5 * q6,
    )
    results = []
    for value, curl, product in zip((q1, q2, q3, q4, q5), chiral, square):
        bulk = bulk_linear * value - bulk_cubic * product + bulk_quartic * trace * value
        results.append((elastic / smoothing) * value - chiral_weight * curl - bulk)
    return jnp.stack(results, axis=1)


def symbol_line(wave, length):
    return 2.0 - 2.0 * jnp.cos(2.0 * math.pi / length * wave.astype(jnp.float32))


def cas_table(length):
    index = jnp.arange(length, dtype=jnp.int32)
    angle = 2.0 * math.pi / length * (index[:, None] * index[None, :] % length).astype(jnp.float32)
    return jnp.cos(angle) + jnp.sin(angle)


def apply_table(table, field, pattern):
    return jnp.einsum(pattern, table, field, precision=lax.Precision.HIGH)


def interp_matrix(arc, centre, target, columns, offset):
    nodes_index = jnp.arange(arc.shape[0], dtype=jnp.int32)

    def pick(where_at):
        return jnp.sum(jnp.where(nodes_index[None, :] == where_at[:, None], arc[None, :], 0.0), axis=1)

    before = pick(centre - 1)
    middle = pick(centre)
    after = pick(centre + 1)
    weight_before = (target - middle) * (target - after) / ((before - middle) * (before - after))
    weight_middle = (target - before) * (target - after) / ((middle - before) * (middle - after))
    weight_after = (target - before) * (target - middle) / ((after - before) * (after - middle))
    column_index = jnp.arange(columns, dtype=jnp.int32)
    matrix = jnp.zeros((centre.shape[0], columns), jnp.float32)
    for shift_by, weight in ((-1, weight_before), (0, weight_middle), (1, weight_after)):
        spot = centre + shift_by - offset
        matrix = matrix + jnp.where(column_index[None, :] == spot[:, None], weight[:, None], 0.0)
    return matrix


def local(images, centre, positions):
    count_img, _, slab, width_x, width_y = images.shape
    groups = lax.axis_size("gz")
    depth = slab * groups
    block = width_x // groups
    parts = chunks if count_img % chunks == 0 else 1
    each = count_img // parts
    wave_x = lax.axis_index("gz") * block + jnp.arange(block, dtype=jnp.int32)
    symbol = symbol_line(jnp.arange(depth, dtype=jnp.int32), depth)[:, None, None]
    symbol = symbol + symbol_line(wave_x, width_x)[None, :, None]
    symbol = symbol + symbol_line(jnp.arange(width_y, dtype=jnp.int32), width_y)[None, None, :]
    multiplier = step_size / ((1.0 + smoothing * symbol) * float(width_x * width_y * depth))
    multiplier = multiplier[:, None, None]
    cas_x = cas_table(width_x).reshape(groups, block, width_x)
    cas_y = cas_table(width_y)
    cas_z = cas_table(depth).reshape(depth, groups, slab)

    pieces = [images[i * each : (i + 1) * each] for i in range(parts)]
    halos = []
    for piece in pieces:
        low = shift_along(z_sources(piece[:, :, slab - 1 :]), "gz", 1, True)
        high = shift_along(z_sources(piece[:, :, :1]), "gz", -1, True)
        halos.append((low, high))
    stepped = []
    for piece, (low, high) in zip(pieces, halos):
        drive = local_drive(piece, low, high)
        spread = apply_table(cas_y, drive, "ky,abzxy->abzxk")
        spread = apply_table(cas_x, spread, "gkx,abzxy->gabzky")
        lines = lax.all_to_all(spread, "gz", split_axis=0, concat_axis=0)
        spectrum = apply_table(cas_z, lines, "wgz,gabzky->wabky") * multiplier
        solved = apply_table(cas_z, spectrum, "wgz,wabky->gabzky")
        gathered = lax.all_to_all(solved, "gz", split_axis=0, concat_axis=0)
        update = apply_table(cas_x, gathered, "gkx,gabzky->abzxy")
        update = apply_table(cas_y, update, "ky,abzxk->abzxy")
        stepped.append((1.0 - step_size * elastic / smoothing) * piece + update)

    single = [part[i : i + 1] for part in stepped for i in range(each)]
    reach = 2
    right = [shift_along(single[i], "img", -1, False) for i in range(reach)]
    left = [shift_along(single[count_img - reach + i], "img", 1, False) for i in range(reach)]
    extended = left + single + right

    total_images = count_img * lax.axis_size("img")
    first_image = lax.axis_index("img") * count_img
    pair_sums = []
    for i in range(count_img):
        gap = extended[reach + i + 1] - extended[reach + i]
        pair_sums.append(jnp.sum(gap * gap))
    sums = jnp.stack(pair_sums)
    global_index = jnp.arange(total_images, dtype=jnp.int32)
    own = global_index // count_img == lax.axis_index("img")
    totals = lax.psum(jnp.where(own, jnp.tile(sums, lax.axis_size("img")), 0.0), ("img", "gz"))
    cells = 5.0 * depth * width_x * width_y
    dist = jnp.where(global_index < total_images - 1, jnp.sqrt(totals / cells + epsilon), 0.0)
    earlier = global_index[None, :] < global_index[:, None]
    arc = jnp.sum(jnp.where(earlier, dist[None, :], 0.0), axis=1)
    target = positions * jnp.sum(dist)
    matrix = interp_matrix(arc, centre, target, count_img + 2 * reach, first_image - reach)
    path = []
    for m in range(count_img):
        terms = [matrix[m, m + d] * extended[m + d] for d in range(2 * reach + 1)]
        path.append(sum(terms[1:], terms[0]))
    return jnp.concatenate(path, axis=0)


def solution(mesh):
    in_specs = (P("img", None, "gz", None, None), P("img"), P("img"))
    out_specs = P("img", None, "gz", None, None)
    return jax.shard_map(local, mesh=mesh, in_specs=in_specs, out_specs=out_specs, check_vma=False)
```

```python
import math

import jax
import jax.numpy as jnp
from jax import lax
from jax.experimental import pallas as pl
from jax.experimental.pallas import tpu as pltpu
from jax.sharding import PartitionSpec as P

elastic = 1.0
chiral_weight = 0.5
bulk_linear = -0.2
bulk_cubic = 0.5
bulk_quartic = 0.1
step_size = 1.0
smoothing = 64.0
epsilon = 1e-06
chunks = 2


def shift_along(block, axis, step, periodic):
    count = lax.axis_size(axis)
    pairs = [(i, i + step) for i in range(count) if 0 <= i + step < count]
    if periodic:
        pairs = [(i, (i + step) % count) for i in range(count)]
    return lax.ppermute(block, axis, pairs)


def z_sources(images):
    return jnp.stack(
        [images[:, 1], images[:, 2], images[:, 4], images[:, 0] - images[:, 3]], axis=1
    )


def local_drive(images, low, high):
    q1, q2, q3, q4, q5 = (images[:, slot] for slot in range(5))
    q6 = -(q1 + q4)

    def grad_x(field):
        return (jnp.roll(field, -1, 2) - jnp.roll(field, 1, 2)) * 0.5

    def grad_y(field):
        return (jnp.roll(field, -1, 3) - jnp.roll(field, 1, 3)) * 0.5

    def grad_z(field, slot):
        padded = jnp.concatenate([low[:, slot], field, high[:, slot]], axis=1)
        return (padded[:, 2:] - padded[:, :-2]) * 0.5

    z2 = grad_z(q2, 0)
    z3 = grad_z(q3, 1)
    z5 = grad_z(q5, 2)
    z14 = grad_z(q1 - q4, 3)
    chiral = (
        2.0 * (grad_y(q3) - z2),
        grad_y(q5) - grad_x(q3) + z14,
        grad_y(q6 - q1) + grad_x(q2) - z5,
        2.0 * (z2 - grad_x(q5)),
        z3 + grad_x(q4 - q6) - grad_y(q2),
    )
    s1 = q1 * q1 + q2 * q2 + q3 * q3
    s4 = q2 * q2 + q4 * q4 + q5 * q5
    trace = s1 + s4 + q3 * q3 + q5 * q5 + q6 * q6
    square = (
        s1 - trace / 3.0,
        q1 * q2 + q2 * q4 + q3 * q5,
        q1 * q3 + q2 * q5 + q3 * q6,
        s4 - trace / 3.0,
        q2 * q3 + q4 * q5 + q5 * q6,
    )
    results = []
    for value, curl, product in zip((q1, q2, q3, q4, q5), chiral, square):
        bulk = bulk_linear * value - bulk_cubic * product + bulk_quartic * trace * value
        results.append((elastic / smoothing) * value - chiral_weight * curl - bulk)
    return jnp.stack(results, axis=1)


def symbol_line(wave, length):
    return 2.0 - 2.0 * jnp.cos(2.0 * math.pi / length * wave.astype(jnp.float32))


def cas_table(length):
    index = jnp.arange(length, dtype=jnp.int32)
    angle = 2.0 * math.pi / length * (index[:, None] * index[None, :] % length).astype(jnp.float32)
    return jnp.cos(angle) + jnp.sin(angle)


def apply_table(table, field, pattern):
    return jnp.einsum(pattern, table, field, precision=lax.Precision.HIGH)


def interp_matrix(arc, centre, target, columns, offset):
    nodes_index = jnp.arange(arc.shape[0], dtype=jnp.int32)

    def pick(where_at):
        return jnp.sum(jnp.where(nodes_index[None, :] == where_at[:, None], arc[None, :], 0.0), axis=1)

    before = pick(centre - 1)
    middle = pick(centre)
    after = pick(centre + 1)
    weight_before = (target - middle) * (target - after) / ((before - middle) * (before - after))
    weight_middle = (target - before) * (target - after) / ((middle - before) * (middle - after))
    weight_after = (target - before) * (target - middle) / ((after - before) * (after - middle))
    column_index = jnp.arange(columns, dtype=jnp.int32)
    matrix = jnp.zeros((centre.shape[0], columns), jnp.float32)
    for shift_by, weight in ((-1, weight_before), (0, weight_middle), (1, weight_after)):
        spot = centre + shift_by - offset
        matrix = matrix + jnp.where(column_index[None, :] == spot[:, None], weight[:, None], 0.0)
    return matrix


def local(images, centre, positions):
    count_img, _, slab, width_x, width_y = images.shape
    groups = lax.axis_size("gz")
    depth = slab * groups
    block = width_x // groups
    parts = chunks if count_img % chunks == 0 else 1
    each = count_img // parts
    wave_x = lax.axis_index("gz") * block + jnp.arange(block, dtype=jnp.int32)
    symbol = symbol_line(jnp.arange(depth, dtype=jnp.int32), depth)[:, None, None]
    symbol = symbol + symbol_line(wave_x, width_x)[None, :, None]
    symbol = symbol + symbol_line(jnp.arange(width_y, dtype=jnp.int32), width_y)[None, None, :]
    multiplier = step_size / ((1.0 + smoothing * symbol) * float(width_x * width_y * depth))
    multiplier = multiplier[:, None, None]
    cas_x = cas_table(width_x).reshape(groups, block, width_x)
    cas_y = cas_table(width_y)
    cas_z = cas_table(depth).reshape(depth, groups, slab)

    pieces = [images[i * each : (i + 1) * each] for i in range(parts)]
    halos = []
    for piece in pieces:
        low = shift_along(z_sources(piece[:, :, slab - 1 :]), "gz", 1, True)
        high = shift_along(z_sources(piece[:, :, :1]), "gz", -1, True)
        halos.append((low, high))
    stepped = []
    for piece, (low, high) in zip(pieces, halos):
        drive = local_drive(piece, low, high)
        spread = apply_table(cas_y, drive, "ky,abzxy->abzxk")
        spread = apply_table(cas_x, spread, "gkx,abzxy->gabzky")
        lines = lax.all_to_all(spread, "gz", split_axis=0, concat_axis=0)
        spectrum = apply_table(cas_z, lines, "wgz,gabzky->wabky") * multiplier
        solved = apply_table(cas_z, spectrum, "wgz,wabky->gabzky")
        gathered = lax.all_to_all(solved, "gz", split_axis=0, concat_axis=0)
        update = apply_table(cas_x, gathered, "gkx,gabzky->abzxy")
        update = apply_table(cas_y, update, "ky,abzxk->abzxy")
        stepped.append((1.0 - step_size * elastic / smoothing) * piece + update)

    reach = 2
    first, last = (stepped[0], stepped[-1]) if each >= reach else (jnp.concatenate(stepped),) * 2
    right = shift_along(first[:reach], "img", -1, False)
    left = shift_along(last[last.shape[0] - reach :], "img", 1, False)
    single = [part[i] for part in stepped for i in range(each)] + [right[0]]

    total_images = count_img * lax.axis_size("img")
    first_image = lax.axis_index("img") * count_img
    pair_sums = []
    for i in range(count_img):
        gap = single[i + 1] - single[i]
        pair_sums.append(jnp.sum(gap * gap))
    devices = lax.axis_size("img") * groups
    sums = jnp.broadcast_to(jnp.stack(pair_sums)[None, :], (devices, count_img))
    sums = lax.all_to_all(sums, ("img", "gz"), split_axis=0, concat_axis=0, tiled=True)
    totals = jnp.sum(sums.reshape(-1, groups, count_img), axis=1).reshape(-1)
    cells = 5.0 * depth * width_x * width_y
    global_index = jnp.arange(total_images, dtype=jnp.int32)
    dist = jnp.where(global_index < total_images - 1, jnp.sqrt(totals / cells + epsilon), 0.0)
    earlier = global_index[None, :] < global_index[:, None]
    arc = jnp.sum(jnp.where(earlier, dist[None, :], 0.0), axis=1)
    target = positions * jnp.sum(dist)
    matrix = interp_matrix(arc, centre, target, count_img + 2 * reach, first_image - reach)
    return mix(matrix, [left] + stepped + [right], images)


def mix_kernel(matrix, *refs):
    *sources, path = refs
    nodes = [source.at[i] for source in sources for i in range(source.shape[0])]
    taken = len(nodes) - path.shape[0] + 1
    for m in range(path.shape[0]):
        total = matrix[m, m] * nodes[m][...]
        for d in range(1, taken):
            total = total + matrix[m, m + d] * nodes[m + d][...]
        path[m] = total


def mix(matrix, sources, like):
    def block(array):
        return pl.BlockSpec(
            (array.shape[0], 1) + array.shape[2:], lambda slot: (0, slot, 0, 0, 0)
        )

    return pl.pallas_call(
        mix_kernel,
        grid=(like.shape[1],),
        in_specs=[pl.BlockSpec(memory_space=pltpu.SMEM)] + [block(s) for s in sources],
        out_specs=block(like),
        out_shape=jax.ShapeDtypeStruct(like.shape, like.dtype),
        compiler_params=pltpu.CompilerParams(vmem_limit_bytes=32 * 2**20),
        cost_estimate=pl.CostEstimate(
            flops=10 * like.size, bytes_accessed=12 * like.size, transcendentals=0
        ),
        name="mix",
    )(matrix, *sources)


def solution(mesh):
    in_specs = (P("img", None, "gz", None, None), P("img"), P("img"))
    out_specs = P("img", None, "gz", None, None)
    return jax.shard_map(local, mesh=mesh, in_specs=in_specs, out_specs=out_specs, check_vma=False)
```

```python
import math

import jax
import jax.numpy as jnp
from jax import lax
from jax.experimental import pallas as pl
from jax.experimental.pallas import tpu as pltpu
from jax.sharding import PartitionSpec as P

elastic = 1.0
chiral_weight = 0.5
bulk_linear = -0.2
bulk_cubic = 0.5
bulk_quartic = 0.1
step_size = 1.0
smoothing = 64.0
epsilon = 1e-06
chunks = 2


def shift_along(block, axis, step, periodic):
    count = lax.axis_size(axis)
    pairs = [(i, i + step) for i in range(count) if 0 <= i + step < count]
    if periodic:
        pairs = [(i, (i + step) % count) for i in range(count)]
    return lax.ppermute(block, axis, pairs)


def z_sources(images):
    return jnp.stack(
        [images[:, 1], images[:, 2], images[:, 4], images[:, 0] - images[:, 3]], axis=1
    )


def local_drive(images, low, high):
    q1, q2, q3, q4, q5 = (images[:, slot] for slot in range(5))
    q6 = -(q1 + q4)

    def grad_x(field):
        return (jnp.roll(field, -1, 2) - jnp.roll(field, 1, 2)) * 0.5

    def grad_y(field):
        return (jnp.roll(field, -1, 3) - jnp.roll(field, 1, 3)) * 0.5

    def grad_z(field, slot):
        padded = jnp.concatenate([low[:, slot], field, high[:, slot]], axis=1)
        return (padded[:, 2:] - padded[:, :-2]) * 0.5

    z2 = grad_z(q2, 0)
    z3 = grad_z(q3, 1)
    z5 = grad_z(q5, 2)
    z14 = grad_z(q1 - q4, 3)
    chiral = (
        2.0 * (grad_y(q3) - z2),
        grad_y(q5) - grad_x(q3) + z14,
        grad_y(q6 - q1) + grad_x(q2) - z5,
        2.0 * (z2 - grad_x(q5)),
        z3 + grad_x(q4 - q6) - grad_y(q2),
    )
    s1 = q1 * q1 + q2 * q2 + q3 * q3
    s4 = q2 * q2 + q4 * q4 + q5 * q5
    trace = s1 + s4 + q3 * q3 + q5 * q5 + q6 * q6
    square = (
        s1 - trace / 3.0,
        q1 * q2 + q2 * q4 + q3 * q5,
        q1 * q3 + q2 * q5 + q3 * q6,
        s4 - trace / 3.0,
        q2 * q3 + q4 * q5 + q5 * q6,
    )
    results = []
    for value, curl, product in zip((q1, q2, q3, q4, q5), chiral, square):
        bulk = bulk_linear * value - bulk_cubic * product + bulk_quartic * trace * value
        results.append((elastic / smoothing) * value - chiral_weight * curl - bulk)
    return jnp.stack(results, axis=1)


def symbol_line(wave, length):
    return 2.0 - 2.0 * jnp.cos(2.0 * math.pi / length * wave.astype(jnp.float32))


def cas_table(length):
    index = jnp.arange(length, dtype=jnp.int32)
    angle = 2.0 * math.pi / length * (index[:, None] * index[None, :] % length).astype(jnp.float32)
    return jnp.cos(angle) + jnp.sin(angle)


def apply_table(table, field, pattern):
    return jnp.einsum(pattern, table, field, precision=lax.Precision.HIGH)


def interp_matrix(arc, centre, target, columns, offset):
    nodes_index = jnp.arange(arc.shape[0], dtype=jnp.int32)

    def pick(where_at):
        return jnp.sum(jnp.where(nodes_index[None, :] == where_at[:, None], arc[None, :], 0.0), axis=1)

    before = pick(centre - 1)
    middle = pick(centre)
    after = pick(centre + 1)
    weight_before = (target - middle) * (target - after) / ((before - middle) * (before - after))
    weight_middle = (target - before) * (target - after) / ((middle - before) * (middle - after))
    weight_after = (target - before) * (target - middle) / ((after - before) * (after - middle))
    column_index = jnp.arange(columns, dtype=jnp.int32)
    matrix = jnp.zeros((centre.shape[0], columns), jnp.float32)
    for shift_by, weight in ((-1, weight_before), (0, weight_middle), (1, weight_after)):
        spot = centre + shift_by - offset
        matrix = matrix + jnp.where(column_index[None, :] == spot[:, None], weight[:, None], 0.0)
    return matrix


def local(images, centre, positions):
    count_img, _, slab, width_x, width_y = images.shape
    groups = lax.axis_size("gz")
    depth = slab * groups
    block = width_x // groups
    parts = chunks if count_img % chunks == 0 else 1
    each = count_img // parts
    wave_x = lax.axis_index("gz") * block + jnp.arange(block, dtype=jnp.int32)
    symbol = symbol_line(jnp.arange(depth, dtype=jnp.int32), depth)[:, None, None]
    symbol = symbol + symbol_line(wave_x, width_x)[None, :, None]
    symbol = symbol + symbol_line(jnp.arange(width_y, dtype=jnp.int32), width_y)[None, None, :]
    multiplier = step_size / ((1.0 + smoothing * symbol) * float(width_x * width_y * depth))
    multiplier = multiplier[:, None, None]
    cas_x = cas_table(width_x).reshape(groups, block, width_x)
    cas_y = cas_table(width_y)
    cas_z = cas_table(depth).reshape(depth, groups, slab)

    pieces = [images[i * each : (i + 1) * each] for i in range(parts)]
    halos = []
    for piece in pieces:
        low = shift_along(z_sources(piece[:, :, slab - 1 :]), "gz", 1, True)
        high = shift_along(z_sources(piece[:, :, :1]), "gz", -1, True)
        halos.append((low, high))
    stepped = []
    for piece, (low, high) in zip(pieces, halos):
        drive = local_drive(piece, low, high)
        spread = apply_table(cas_y, drive, "ky,abzxy->abzxk")
        spread = apply_table(cas_x, spread, "gkx,abzxy->gabzky")
        lines = lax.all_to_all(spread, "gz", split_axis=0, concat_axis=0)
        spectrum = apply_table(cas_z, lines, "wgz,gabzky->wabky") * multiplier
        solved = apply_table(cas_z, spectrum, "wgz,wabky->gabzky")
        gathered = lax.all_to_all(solved, "gz", split_axis=0, concat_axis=0)
        update = apply_table(cas_x, gathered, "gkx,gabzky->abzxy")
        update = apply_table(cas_y, update, "ky,abzxk->abzxy")
        stepped.append((1.0 - step_size * elastic / smoothing) * piece + update)

    reach = 2
    first, last = (stepped[0], stepped[-1]) if each >= reach else (jnp.concatenate(stepped),) * 2
    right = shift_along(first[:reach], "img", -1, False)
    left = shift_along(last[last.shape[0] - reach :], "img", 1, False)
    single = [part[i] for part in stepped for i in range(each)] + [right[0]]

    total_images = count_img * lax.axis_size("img")
    first_image = lax.axis_index("img") * count_img
    pair_sums = []
    for i in range(count_img):
        gap = single[i + 1] - single[i]
        pair_sums.append(jnp.sum(gap * gap))
    devices = lax.axis_size("img") * groups
    sums = jnp.broadcast_to(jnp.stack(pair_sums)[None, :], (devices, count_img))
    sums = lax.all_to_all(sums, ("img", "gz"), split_axis=0, concat_axis=0, tiled=True)
    totals = jnp.sum(sums.reshape(-1, groups, count_img), axis=1).reshape(-1)
    cells = 5.0 * depth * width_x * width_y
    global_index = jnp.arange(total_images, dtype=jnp.int32)
    dist = jnp.where(global_index < total_images - 1, jnp.sqrt(totals / cells + epsilon), 0.0)
    earlier = global_index[None, :] < global_index[:, None]
    arc = jnp.sum(jnp.where(earlier, dist[None, :], 0.0), axis=1)
    target = positions * jnp.sum(dist)
    matrix = interp_matrix(arc, centre, target, count_img + 2 * reach, first_image - reach)
    return mix(matrix, [left] + stepped + [right], images)


def mix_kernel(matrix, *refs):
    *sources, path = refs
    nodes = [source.at[i] for source in sources for i in range(source.shape[0])]
    taken = len(nodes) - path.shape[0] + 1
    for m in range(path.shape[0]):
        total = matrix[m, m] * nodes[m][...]
        for d in range(1, taken):
            total = total + matrix[m, m + d] * nodes[m + d][...]
        path[m] = total


def mix(matrix, sources, like):
    def block(array):
        return pl.BlockSpec(
            (array.shape[0], 1, 1) + array.shape[3:], lambda slot, z: (0, slot, z, 0, 0)
        )

    return pl.pallas_call(
        mix_kernel,
        grid=like.shape[1:3],
        in_specs=[pl.BlockSpec(memory_space=pltpu.SMEM)] + [block(s) for s in sources],
        out_specs=block(like),
        out_shape=jax.ShapeDtypeStruct(like.shape, like.dtype),
        compiler_params=pltpu.CompilerParams(vmem_limit_bytes=32 * 2**20),
        cost_estimate=pl.CostEstimate(
            flops=10 * like.size, bytes_accessed=12 * like.size, transcendentals=0
        ),
        name="mix",
    )(matrix, *sources)


def solution(mesh):
    in_specs = (P("img", None, "gz", None, None), P("img"), P("img"))
    out_specs = P("img", None, "gz", None, None)
    return jax.shard_map(local, mesh=mesh, in_specs=in_specs, out_specs=out_specs, check_vma=False)
```
